256 devices in a mesh: aux: 8 (over z_hi, y), pair: 32 (over x, z_lo, core).
Axes of the slice: x: 4, y: 4, z: 8 (z_hi: 2, z_lo: 4; z = z_hi * 4 + z_lo), core: 2. Of those that a mesh axis runs over, the one named last changes fastest.
Arguments:
- density: bfloat16 [28800, 28800], P('aux', 'pair'), may hold values from -0.03125 to 0.03125
- cholesky: bfloat16 [512, 28800], P('pair', 'aux'), may hold values from -6 to 6
- virtual_orbitals: bfloat16 [3000, 1800], P('aux'), may hold values from -0.125 to 0.125
- occupied_orbitals: bfloat16 [128, 16], replicated, may hold values from -1.5 to 1.5
Outputs:
- back_transformed: bfloat16 [512, 128, 3000], P('pair', None, 'aux')
- lagrangian: float32 [16, 16], P(None, 'aux')
The draws below stay inside these ranges and needn't reach their ends.
All inputs are finite; a program needn't handle non-finite values.
Results may differ from the reference program's by a relative error of at most 0.0057.
Values may be sent and summed in bfloat16 or wider, within the bound.
A program may use at most 64 MiB of HBM per device.

```python
import jax
import jax.numpy as jnp

NVIR = 1800
NAO = 3000
NCHOL = 512
NOCC = 16
AO_ROWS = 128
PAIRS = 28800


def block_levels(stream_key, shape, split, low, top_value):
    def one(position, blocks):
        steps = jax.random.uniform(jax.random.fold_in(jax.random.fold_in(stream_key, 6), position), (blocks,), jnp.float32, low / len(split), top_value / len(split))
        return jnp.repeat(jnp.exp(steps), shape[position] // blocks).reshape((-1,) + (1,) * (len(shape) - position - 1))

    factor_of = one(*split[0])
    for cut in split[1:]:
        factor_of = factor_of * one(*cut)
    return factor_of


def centred(own_key, extent, scale, limit, split=(), held_as=jnp.bfloat16):
    level = block_levels(own_key, extent, split, -0.22, 0.18) if split else 1.0
    array = jax.random.normal(own_key, extent, jnp.float32) * scale * level
    return jnp.minimum(jnp.maximum(array, -limit), limit).astype(held_as)


def setup_inputs(seed: int = 0) -> dict:
    key_list = jax.random.split(jax.random.key(seed), 5)
    density = centred(key_list[0], (PAIRS, PAIRS), PAIRS ** -0.5, 0.03125, ((0, 8), (1, 32)))
    cholesky = centred(key_list[1], (NCHOL, PAIRS), 1.0, 6.0, ((0, 32), (1, 8)))
    virtual_orbitals = centred(key_list[2], (NAO, NVIR), NVIR ** -0.5, 0.125, ((0, 8),))
    occupied_orbitals = centred(key_list[3], (AO_ROWS, NOCC), NOCC ** -0.5, 1.5)
    return dict(density=density, cholesky=cholesky, virtual_orbitals=virtual_orbitals, occupied_orbitals=occupied_orbitals)


def reference(density, cholesky, virtual_orbitals, occupied_orbitals):
    gamma = jnp.dot(cholesky, density, preferred_element_type=jnp.float32).astype(jnp.bfloat16)
    flat = gamma.reshape(NCHOL * NOCC, NVIR)
    half_done = jnp.dot(flat, virtual_orbitals.T, preferred_element_type=jnp.float32).astype(jnp.bfloat16)
    half_done = half_done.reshape(NCHOL, NOCC, NAO)
    back_transformed = jnp.einsum("mi,kin->kmn", occupied_orbitals.astype(jnp.float32), half_done.astype(jnp.float32)).astype(jnp.bfloat16)
    blocked = gamma.reshape(NCHOL, NOCC, NVIR).astype(jnp.float32)
    vectors = cholesky.reshape(NCHOL, NOCC, NVIR).astype(jnp.float32)
    lagrangian = jnp.einsum("kib,kjb->ij", blocked, vectors) / NCHOL
    return back_transformed, lagrangian
```

```python
import jax
import jax.numpy as jnp
from jax import lax
from jax.experimental import pallas as pl
from jax.experimental.pallas import tpu as pltpu
from jax.sharding import PartitionSpec as P

MESH = pl.DeviceIdType.MESH
F32 = jnp.float32
BF16 = jnp.bfloat16
NT = (((1,), (1,)), ((), ()))

NX, NY, NZ, NC = 4, 4, 4, 2
ROWS = 16
CUTS = (0, 224, 448, 672, 900)
WIDE = 256
COLUMN = (0, 1, 3, 2)
BACK = (0, 2, 1, 3)
NCHOL = 512


def kernel(
    dt_hbm, chol_hbm, virt_hbm, occ_hbm, out_ref, lag_ref,
    gath, dt, virt, occ, virtp, lc, weights, part, fromy, summed, owned, gamma, half, lagrow, lagmine, lagall,
    local_sem, bulk_sem, block_sem, y_sem, own_sem, g_sem, lag_sem,
    send_block, send_y, send_own, send_g, send_lag,
):
    aux, pair = lax.axis_index("aux"), lax.axis_index("pair")
    zh, y = aux // NY, aux % NY
    x, zl, c = pair // (NZ * NC), (pair // NC) % NZ, pair % NC
    me = c * NZ + zl

    def device(zh_, y_, x_, zl_, c_):
        return (zh_ * NY + y_, (x_ * NZ + zl_) * NC + c_)

    barrier = pltpu.get_barrier_semaphore()
    own_place = zh * 32 + pair

    def greet(t, carry):
        @pl.when(t != own_place)
        def _():
            pl.semaphore_signal(barrier, inc=1, device_id=((t // 32) * NY + y, t % 32), device_id_type=MESH)

        return carry

    lax.fori_loop(0, 64, greet, 0)
    for dy in range(1, NY):
        pl.semaphore_signal(barrier, inc=1, device_id=(zh * NY + (y + dy) % NY, pair), device_id_type=MESH)

    own = pltpu.make_async_copy(chol_hbm, gath.at[0, me], local_sem.at[0])
    own.start()
    load_virt = pltpu.make_async_copy(virt_hbm, virt, local_sem.at[1])
    load_virt.start()
    load_occ = pltpu.make_async_copy(occ_hbm, occ, local_sem.at[2])
    load_occ.start()
    load_dt = pltpu.make_async_copy(dt_hbm, dt, bulk_sem)
    load_dt.start()
    own.wait()
    pl.semaphore_wait(barrier, 66)

    def block(src_k, dst_k, j, target):
        return pltpu.make_async_remote_copy(
            src_ref=gath.at[src_k, j], dst_ref=gath.at[dst_k, j], send_sem=send_block,
            recv_sem=block_sem.at[dst_k, j], device_id=target, device_id_type=MESH,
        )

    right = device(zh, y, (x + 1) % NX, zl, c)
    left = device(zh, y, (x + NX - 1) % NX, zl, c)
    sibling = device(zh, y, x, zl, 1 - c)
    up = device(zh, y, x, (zl + 1) % NZ, c)
    down = device(zh, y, x, (zl + NZ - 1) % NZ, c)

    def arrived(k, j):
        pltpu.make_async_copy(gath.at[k, j], gath.at[k, j], block_sem.at[k, j]).wait()

    pick = lambda a, b, c_, d: jnp.where(zl == 0, a, jnp.where(zl == 1, b, jnp.where(zl == 2, c_, d)))
    order = (zl, pick(1, 2, 3, 2), pick(2, 0, 1, 1), pick(3, 3, 0, 0))

    def along_x(j):
        block(0, 2, j, right).start()
        block(0, 1, j, left).start()
        block(0, 0, j, sibling).start()

    def own_column(q):
        j = c * NZ + order[q]
        if q == 0:
            @pl.when(zl < NZ - 1)
            def _():
                block(0, 0, j, up).start()

            @pl.when(zl > 0)
            def _():
                block(0, 0, j, down).start()
        else:
            arrived(0, j)

            @pl.when((order[q] < zl) & (zl < NZ - 1))
            def _():
                block(0, 0, j, up).start()

            @pl.when((order[q] > zl) & (zl > 0))
            def _():
                block(0, 0, j, down).start()

        along_x(j)

    def beside(q):
        j = c * NZ + order[q]
        arrived(1, j)
        if q % 2 == 1:
            block(1, 3, j, left).start()
        block(1, 1, j, sibling).start()
        arrived(2, j)
        if q % 2 == 0:
            block(2, 3, j, right).start()
        block(2, 2, j, sibling).start()

    def opposite(q):
        j = c * NZ + order[q]
        arrived(3, j)
        block(3, 3, j, sibling).start()

    def from_sibling(k):
        for z in range(NZ):
            arrived(k, (1 - c) * NZ + z)

    def product(k, n):
        rows = gath[pl.ds(k, n)].reshape(n * 128, 3600)
        for cut in range(NY):
            width = CUTS[cut + 1] - CUTS[cut]
            value = lax.dot_general(rows, dt[pl.ds(CUTS[cut], width), :], NT, preferred_element_type=F32).astype(BF16)
            for m in range(n):
                part[k + m, cut, :, 0:width] = value[m * 128 : (m + 1) * 128]
        for m in range(n):
            for dy in range(1, NY):
                over_y(k + m, dy).start()

    def over_y(k, dy):
        to = (y + dy) % NY
        return pltpu.make_async_remote_copy(
            src_ref=part.at[k, to], dst_ref=fromy.at[k, dy - 1], send_sem=send_y, recv_sem=y_sem.at[k, dy - 1],
            device_id=(zh * NY + to, pair), device_id_type=MESH,
        )

    def to_owner(k, t):
        tz, j = t // 8, t % 8
        return pltpu.make_async_remote_copy(
            src_ref=summed.at[k, j], dst_ref=owned.at[BACK[k], zh, me], send_sem=send_own, recv_sem=own_sem.at[BACK[k]],
            device_id=device(tz, y, (x + COLUMN[k]) % NX, j % NZ, j // NZ), device_id_type=MESH,
        )

    def sum_y(k):
        total = part[k, y].astype(F32)
        for dy in range(1, NY):
            over_y(k, dy).wait_recv()
            total = total + fromy[k, dy - 1].astype(F32)
        summed[k] = total.astype(BF16).reshape(8, ROWS, WIDE)

        def send(t, carry):
            t = (t + zh * 8 + me) % 16
            if k == 0:
                @pl.when(t != zh * 8 + me)
                def _():
                    to_owner(k, t).start()

                @pl.when(t == zh * 8 + me)
                def _():
                    pltpu.make_async_copy(summed.at[k, me], owned.at[0, zh, me], own_sem.at[0]).start()
            else:
                to_owner(k, t).start()
            return carry

        lax.fori_loop(0, 16, send, 0)

    def gather_y(k, dy):
        return pltpu.make_async_remote_copy(
            src_ref=gamma.at[k, y], dst_ref=gamma.at[k, y], send_sem=send_g, recv_sem=g_sem.at[k, dy - 1],
            device_id=(zh * NY + (y + dy) % NY, pair), device_id_type=MESH,
        )

    def complete(k):
        pltpu.make_async_copy(owned.at[k], owned.at[k], own_sem.at[k]).wait()
        gamma[k, y] = (owned[k, 0].astype(F32) + owned[k, 1].astype(F32)).astype(BF16)
        for dy in range(1, NY):
            gather_y(k, dy).start()

    def transform(k):
        for dy in range(1, NY):
            gather_y(k, dy).wait_recv()
        total = jnp.zeros((64, 375), F32)
        for h in range(2):
            for cut in range(NY):
                total = total + jnp.dot(
                    gamma[k, cut, pl.ds(4 * h, 4)].reshape(64, WIDE), virtp[4 * h + cut], preferred_element_type=F32
                )
        half[k] = total
        for z in range(NZ):
            i = ((x + COLUMN[k]) % NX) * NZ + z
            for j in range(2):
                terms = jnp.zeros((ROWS, WIDE), F32)
                for h in range(2):
                    for cut in range(NY):
                        terms = terms + gamma[k, cut, 4 * h + z].astype(F32) * lc[j, 4 * h + cut]
                terms = terms[:, :128] + terms[:, 128:]
                lagrow[j, pl.ds(i, 1), :] = jnp.sum(terms, axis=0, keepdims=True)

    own_column(0)

    part[:, :, :, 128:256] = jnp.zeros((4, NY, 128, 128), BF16)
    virtp[...] = jnp.zeros(virtp.shape, BF16)
    lc[...] = jnp.zeros(lc.shape, F32)
    lagmine[...] = jnp.zeros(lagmine.shape, F32)
    load_virt.wait()
    load_occ.wait()
    for h in range(2):
        for cut in range(NY):
            width = CUTS[cut + 1] - CUTS[cut]
            start = h * 900 + CUTS[cut]
            first = start // 8 * 8
            value = virt[first : start + width, :].astype(F32)
            virtp[4 * h + cut, 0:width, :] = value[start - first :].astype(BF16)
    mine = gath[0, me].astype(F32)
    for j in range(2):
        for h in range(2):
            for cut in range(NY):
                width = CUTS[cut + 1] - CUTS[cut]
                start = j * 1800 + h * 900 + CUTS[cut]
                lc[j, 4 * h + cut, :, 0:width] = mine[:, start : start + width]
    for k in range(4):
        for z in range(NZ):
            i = ((x + COLUMN[k]) % NX) * NZ + z
            row = occ[pl.ds(i, 1), :]
            weights[pl.ds(k * 64 + z * 16, 16), :] = jnp.broadcast_to(row, (16, 128)).astype(BF16)

    own_column(1)
    beside(0)
    own_column(2)
    beside(1)
    own_column(3)
    beside(2)
    from_sibling(0)
    load_dt.wait()
    product(0, 1)
    beside(3)
    from_sibling(1)
    from_sibling(2)
    product(1, 2)
    sum_y(0)
    for q in range(4):
        opposite(q)
    sum_y(1)
    sum_y(2)
    complete(0)
    from_sibling(3)
    product(3, 1)
    complete(1)
    complete(2)
    transform(0)
    sum_y(3)
    transform(1)
    transform(2)
    complete(3)
    transform(3)

    lagmine[0:2, 0:16] = jnp.sum(lagrow[...], axis=-1) * (1.0 / NCHOL)

    def share(t, carry):
        to = (pair + t) % 32
        pltpu.make_async_remote_copy(
            src_ref=lagmine, dst_ref=lagall.at[pair], send_sem=send_lag, recv_sem=lag_sem,
            device_id=(aux, to), device_id_type=MESH,
        ).start()
        return carry

    pltpu.make_async_copy(lagmine, lagall.at[pair], lag_sem).start()
    lax.fori_loop(1, 32, share, 0)

    turned = half[...].reshape(256, 375).astype(BF16).astype(F32).T
    row = lax.broadcasted_iota(jnp.int32, (ROWS, 256), 0)
    lane = lax.broadcasted_iota(jnp.int32, (ROWS, 256), 1)
    keep = (lane % ROWS) == row
    for start in range(0, 375, 64):
        n = min(64, 375 - start)
        spread = jnp.where(keep[None], turned[start : start + n][:, None, :], 0.0).astype(BF16)
        value = jnp.dot(spread.reshape(n * ROWS, 256), weights[...], preferred_element_type=F32)
        out_ref[start : start + n] = value.astype(BF16).reshape(n, ROWS, 128)

    pltpu.make_async_copy(lagall, lagall, lag_sem).wait()
    lag_ref[...] = jnp.sum(lagall[...], axis=0)[0:2, 0:16]

    sent = 28 + jnp.where(zl < NZ - 1, zl + 1, 0) + jnp.where(zl > 0, NZ - zl, 0)

    def left_block(t, carry):
        block(0, 0, 0, sibling).wait_send()
        return carry

    lax.fori_loop(0, sent, left_block, 0)

    def left_y(t, carry):
        over_y(0, 1).wait_send()
        gather_y(0, 1).wait_send()
        return carry

    lax.fori_loop(0, 12, left_y, 0)

    def left_own(t, carry):
        to_owner(1, 0).wait_send()
        return carry

    lax.fori_loop(0, 63, left_own, 0)

    def left_lag(t, carry):
        pltpu.make_async_remote_copy(
            src_ref=lagmine, dst_ref=lagall.at[pair], send_sem=send_lag, recv_sem=lag_sem,
            device_id=sibling, device_id_type=MESH,
        ).wait_send()
        return carry

    lax.fori_loop(0, 31, left_lag, 0)


def on_device(density, cholesky, virtual_orbitals, occupied_orbitals):
    anywhere = pl.BlockSpec(memory_space=pl.ANY)
    vmem = pl.BlockSpec(memory_space=pltpu.VMEM)
    dma = pltpu.SemaphoreType.DMA
    back, lagrangian = pl.pallas_call(
        kernel,
        name="density",
        out_shape=(jax.ShapeDtypeStruct((375, ROWS, 128), BF16), jax.ShapeDtypeStruct((2, 16), F32)),
        in_specs=[anywhere] * 4,
        out_specs=(vmem, vmem),
        scratch_shapes=[
            pltpu.VMEM((4, 8, ROWS, 3600), BF16),
            pltpu.VMEM((900, 3600), BF16),
            pltpu.VMEM((1800, 375), BF16),
            pltpu.VMEM((16, 128), F32),
            pltpu.VMEM((8, WIDE, 375), BF16),
            pltpu.VMEM((2, 8, ROWS, WIDE), F32),
            pltpu.VMEM((256, 128), BF16),
            pltpu.VMEM((4, NY, 128, WIDE), BF16),
            pltpu.VMEM((4, NY - 1, 128, WIDE), BF16),
            pltpu.VMEM((4, 8, ROWS, WIDE), BF16),
            pltpu.VMEM((4, 2, 8, ROWS, WIDE), BF16),
            pltpu.VMEM((4, NY, 8, ROWS, WIDE), BF16),
            pltpu.VMEM((4, 64, 375), F32),
            pltpu.VMEM((2, 16, 128), F32),
            pltpu.VMEM((8, 128), F32),
            pltpu.VMEM((32, 8, 128), F32),
            dma((3,)),
            dma,
            dma((4, 8)),
            dma((4, NY - 1)),
            dma((4,)),
            dma((4, NY - 1)),
            dma,
            dma,
            dma,
            dma,
            dma,
            dma,
        ],
        compiler_params=pltpu.CompilerParams(collective_id=0, has_side_effects=True, vmem_limit_bytes=56 * 2**20),
        cost_estimate=pl.CostEstimate(flops=5 * 10**9, bytes_accessed=12 * 2**20, transcendentals=0),
    )(density.T, cholesky, virtual_orbitals.T, occupied_orbitals.T.astype(F32))
    return back.transpose(1, 2, 0), lagrangian.T


def solution(mesh):
    return jax.shard_map(
        on_device,
        mesh=mesh,
        in_specs=(P("aux", "pair"), P("pair", "aux"), P("aux", None), P()),
        out_specs=(P("pair", None, "aux"), P(None, "aux")),
        check_vma=False,
    )
```

```python
import jax
import jax.numpy as jnp
from jax import lax
from jax.experimental import pallas as pl
from jax.experimental.pallas import tpu as pltpu
from jax.sharding import PartitionSpec as P

MESH = pl.DeviceIdType.MESH
F32 = jnp.float32
BF16 = jnp.bfloat16
NT = (((1,), (1,)), ((), ()))

NX, NY, NZ, NC = 4, 4, 4, 2
ROWS = 16
CUT = 224
LAST = 228
WIDE = 256
HALVES = (0, 1792, 3600)
NCHOL = 512


def kernel(
    dt_hbm, chol_hbm, virt_hbm, occ_hbm, out_ref, lag_ref,
    gath, dt, virt, occ, occ32, virtp, lc, weights, part, mine, fromy, summed, owned, gamma, turned, lagrow, lagmine, lagall,
    local_sem, bulk_sem, block_sem, y_sem, own_sem, g_sem, lag_sem, plane_sem,
    send_first, send_second, send_y, send_own, send_g, send_lag,
):
    aux, pair = lax.axis_index("aux"), lax.axis_index("pair")
    zh, y = aux // NY, aux % NY
    x, zl, c = pair // (NZ * NC), (pair // NC) % NZ, pair % NC
    me = c * NX + x
    rows_of = (zl, zl + 1 - 2 * lax.rem(zl, 2), lax.rem(zl + 2, NZ), NZ - 1 - zl)

    auxes = [[(zh * NY if d == 0 else (1 - zh) * NY) + lax.rem(y + e, NY) for e in range(NY)] for d in range(2)]
    xs = [lax.rem(x + d, NX) for d in range(NX)]
    zs = [lax.rem(zl + d, NZ) for d in range(NZ)]
    cs = [c, 1 - c]

    def device(dzh=0, dy=0, dx=0, dz=0, dc=0):
        return (auxes[dzh][dy], (xs[dx] * NZ + zs[dz]) * NC + cs[dc])

    right, left, sibling, up, down = device(dx=1), device(dx=3), device(dc=1), device(dz=1), device(dz=3)
    across = device(dzh=1)

    barrier = pltpu.get_barrier_semaphore()
    friends = [right, left, sibling, up, down, across] + [device(dy=e) for e in range(1, NY)]
    for friend in friends:
        pl.semaphore_signal(barrier, inc=1, device_id=friend, device_id_type=MESH)

    own = pltpu.make_async_copy(chol_hbm, gath.at[0, c * NX], local_sem.at[0])
    own.start()
    load_occ = pltpu.make_async_copy(occ_hbm, occ, local_sem.at[2])
    load_occ.start()
    load_virt = pltpu.make_async_copy(virt_hbm, virt, local_sem.at[1])
    load_virt.start()
    load_dt = pltpu.make_async_copy(dt_hbm, dt, bulk_sem)
    load_dt.start()

    def block(src, dst, h, target):
        cols = pl.ds(HALVES[h], HALVES[h + 1] - HALVES[h])
        return pltpu.make_async_remote_copy(
            src_ref=gath.at[src[0], src[1], :, cols], dst_ref=gath.at[dst[0], dst[1], :, cols],
            send_sem=(send_first, send_second)[h], recv_sem=block_sem.at[h, dst[0], dst[1]],
            device_id=target, device_id_type=MESH,
        )

    def arrived(q, j, h):
        block((q, j), (q, j), h, sibling).wait_recv()

    def xor(a, b):
        return a + b - 2 * (lax.rem(a, 2) * lax.rem(b, 2)) - 4 * ((a // 2) * (b // 2))

    mine_first = c * NX

    def along_z(s_, h):
        above, below = zl + s_, zl - s_

        @pl.when(above < NZ)
        def _():
            at = xor(zl, above)
            if s_ > 0:
                arrived(at, mine_first, h)

            @pl.when(zl > 0)
            def _():
                block((at, mine_first), (xor(zl - 1, above), mine_first), h, down).start()

        @pl.when(below >= 0)
        def _():
            at = xor(zl, below)
            if s_ > 0:
                arrived(at, mine_first, h)

            @pl.when(zl < NZ - 1)
            def _():
                block((at, mine_first), (xor(zl + 1, below), mine_first), h, up).start()

    def own_column(q, h):
        along_z(q, h)
        block((q, mine_first), (q, mine_first + 3), h, right).start()
        block((q, mine_first), (q, mine_first + 1), h, left).start()
        block((q, mine_first), (q, mine_first), h, sibling).start()

    def beside(q, h):
        for g, other, target in ((1, 0, left), (3, 1, right)):
            j = mine_first + g
            arrived(q, j, h)
            if q % 2 == 1 - other:
                block((q, j), (q, mine_first + 2), h, target).start()
            block((q, j), (q, j), h, sibling).start()

    def opposite(q):
        j = mine_first + 2
        for h in range(2):
            arrived(q, j, h)
            block((q, j), (q, j), h, sibling).start()

    def from_sibling(q):
        for g in range(NX):
            for h in range(2):
                arrived(q, (1 - c) * NX + g, h)
        pl.semaphore_signal(plane_sem.at[q], inc=1, device_id=across, device_id_type=MESH)

    def over_y(k, t):
        return pltpu.make_async_remote_copy(
            src_ref=part.at[k, t], dst_ref=fromy.at[k, t], send_sem=send_y, recv_sem=y_sem.at[k, t],
            device_id=device(dy=t + 1), device_id_type=MESH,
        )

    def product(k, t):
        rows = gath[k].reshape(128, 3600)
        cut = lax.rem(y + 1 + t, NY)
        pairs = dt[pl.ds(pl.multiple_of(cut * CUT, 16), LAST), :]
        value = lax.dot_general(rows, pairs, NT, preferred_element_type=F32)
        if t < NY - 1:
            part[k, t, :, 0:LAST] = value.astype(BF16)
            over_y(k, t).start()
        else:
            mine[k, :, 0:LAST] = value

    def to_owner(k, dzh, g, dc):
        return pltpu.make_async_remote_copy(
            src_ref=summed.at[k, cs[dc] * NX + g], dst_ref=owned.at[k, zh, me],
            send_sem=send_own, recv_sem=own_sem.at[k],
            device_id=(auxes[dzh][0], (xs[g] * NZ + rows_of[k]) * NC + cs[dc]), device_id_type=MESH,
        )

    def sum_y(k):
        total = mine[k]
        for t in range(NY - 1):
            over_y(k, t).wait_recv()
            total = total + fromy[k, t].astype(F32)
        summed[k] = total.astype(BF16).reshape(8, ROWS, WIDE)
        pl.semaphore_wait(plane_sem.at[k], 1)
        for dzh in (1, 0):
            for g in (2, 1, 3, 0):
                for dc in range(NC):
                    if k == 0 and g == 0 and dc == 0 and dzh == 0:
                        pltpu.make_async_copy(summed.at[k, c * NX], owned.at[0, zh, me], own_sem.at[0]).start()
                    else:
                        to_owner(k, dzh, g, dc).start()

    def gather_y(k, t):
        return pltpu.make_async_remote_copy(
            src_ref=gamma.at[k, y], dst_ref=gamma.at[k, y], send_sem=send_g, recv_sem=g_sem.at[k, t],
            device_id=device(dy=t + 1), device_id_type=MESH,
        )

    def complete(k):
        pltpu.make_async_copy(owned.at[k], owned.at[k], own_sem.at[k]).wait()
        gamma[k, y] = (owned[k, 0].astype(F32) + owned[k, 1].astype(F32)).astype(BF16)
        for t in range(NY - 1):
            gather_y(k, t).start()

    def transform(k):
        for t in range(NY - 1):
            gather_y(k, t).wait_recv()
        total = jnp.zeros((64, 375), F32)
        for h in range(2):
            for cut in range(NY):
                total = total + jnp.dot(
                    gamma[k, cut, pl.ds(4 * h, 4)].reshape(64, WIDE), virtp[4 * h + cut], preferred_element_type=F32
                )
        turned[:, k * 64 : (k + 1) * 64] = total.astype(BF16).astype(F32).T
        for z in range(NZ):
            i = z * NZ + rows_of[k]
            for j in range(2):
                terms = jnp.zeros((ROWS, WIDE), F32)
                for h in range(2):
                    for cut in range(NY):
                        terms = terms + gamma[k, cut, 4 * h + z].astype(F32) * lc[j, 4 * h + cut]
                terms = terms[:, :128] + terms[:, 128:]
                lagrow[j, pl.ds(i, 1), :] = jnp.sum(terms, axis=0, keepdims=True)

    def pad_virtual(h):
        for cut in range(NY):
            width = LAST if cut == NY - 1 else CUT
            start = h * 900 + cut * CUT
            first = start // 8 * 8
            value = virt[first : start + width, :].astype(F32)
            virtp[4 * h + cut, 0:width, :] = value[start - first :].astype(BF16)

    own.wait()
    virtp[...] = jnp.zeros(virtp.shape, BF16)
    pl.semaphore_wait(barrier, len(friends))
    own_column(0, 0)
    own_column(0, 1)

    part[:, :, :, 128:WIDE] = jnp.zeros((4, NY - 1, 128, WIDE - 128), BF16)
    mine[:, :, 128:WIDE] = jnp.zeros((4, 128, WIDE - 128), F32)
    lc[...] = jnp.zeros(lc.shape, F32)
    lagmine[...] = jnp.zeros(lagmine.shape, F32)
    load_occ.wait()
    occ32[...] = occ[...].astype(F32)
    for k in range(4):
        for z in range(NZ):
            row = occ32[pl.ds(z * NZ + rows_of[k], 1), :]
            weights[pl.ds(k * 64 + z * 16, 16), :] = jnp.broadcast_to(row, (16, 128)).astype(BF16)

    own_column(1, 0)
    beside(0, 0)
    own_column(1, 1)
    beside(0, 1)
    load_virt.wait()
    pad_virtual(0)
    own_column(2, 0)
    own_column(2, 1)
    opposite(0)
    beside(1, 0)
    beside(1, 1)
    pad_virtual(1)
    own_column(3, 0)
    own_column(3, 1)
    own_block = gath[0, c * NX].astype(F32)
    for j in range(2):
        for h in range(2):
            for cut in range(NY):
                width = LAST if cut == NY - 1 else CUT
                start = j * 1800 + h * 900 + cut * CUT
                lc[j, 4 * h + cut, :, 0:width] = own_block[:, start : start + width]
    from_sibling(0)
    load_dt.wait()
    product(0, 0)
    beside(2, 0)
    product(0, 1)
    beside(2, 1)
    product(0, 2)
    opposite(1)
    product(0, 3)
    beside(3, 0)
    from_sibling(1)
    product(1, 0)
    beside(3, 1)
    product(1, 1)
    product(1, 2)
    opposite(2)
    product(1, 3)
    sum_y(0)
    from_sibling(2)
    product(2, 0)
    product(2, 1)
    opposite(3)
    product(2, 2)
    product(2, 3)
    sum_y(1)
    from_sibling(3)
    for t in range(NY):
        product(3, t)
    complete(0)
    sum_y(2)
    complete(1)
    sum_y(3)
    transform(0)
    complete(2)
    transform(1)
    transform(2)
    complete(3)
    transform(3)

    lagmine[0:2, 0:16] = jnp.sum(lagrow[...], axis=-1) * (1.0 / NCHOL)

    def share(t):
        return pltpu.make_async_remote_copy(
            src_ref=lagmine, dst_ref=lagall.at[pair], send_sem=send_lag, recv_sem=lag_sem,
            device_id=(aux, lax.rem(pair + t, 32)), device_id_type=MESH,
        )

    def start_share(t, carry):
        share(t).start()
        return carry

    pltpu.make_async_copy(lagmine, lagall.at[pair], lag_sem).start()
    lax.fori_loop(1, 32, start_share, 0)

    row = lax.broadcasted_iota(jnp.int32, (ROWS, 256), 0)
    lane = lax.broadcasted_iota(jnp.int32, (ROWS, 256), 1)
    keep = (lane % ROWS) == row
    for start in range(0, 375, 64):
        n = min(64, 375 - start)
        spread = jnp.where(keep[None], turned[start : start + n][:, None, :], 0.0).astype(BF16)
        value = jnp.dot(spread.reshape(n * ROWS, 256), weights[...], preferred_element_type=F32)
        out_ref[start : start + n] = value.astype(BF16).reshape(n, ROWS, 128)

    pltpu.make_async_copy(lagall, lagall, lag_sem).wait()
    lag_ref[...] = jnp.sum(lagall[...], axis=0)[0:2, 0:16]

    sent = 28 + jnp.where(zl < NZ - 1, zl + 1, 0) + jnp.where(zl > 0, NZ - zl, 0)

    def left_block(t, carry):
        block((0, 0), (0, 0), 0, sibling).wait_send()
        block((0, 0), (0, 0), 1, sibling).wait_send()
        return carry

    def left_y(t, carry):
        over_y(0, 0).wait_send()
        gather_y(0, 0).wait_send()
        return carry

    def left_own(t, carry):
        to_owner(1, 0, 0, 0).wait_send()
        return carry

    def left_lag(t, carry):
        share(1).wait_send()
        return carry

    lax.fori_loop(0, sent, left_block, 0)
    lax.fori_loop(0, 12, left_y, 0)
    lax.fori_loop(0, 63, left_own, 0)
    lax.fori_loop(0, 31, left_lag, 0)


def on_device(density, cholesky, virtual_orbitals, occupied_orbitals):
    hbm = pl.BlockSpec(memory_space=pltpu.HBM)
    vmem = pl.BlockSpec(memory_space=pltpu.VMEM)
    dma = pltpu.SemaphoreType.DMA
    back, lagrangian = pl.pallas_call(
        kernel,
        name="density",
        out_shape=(jax.ShapeDtypeStruct((375, ROWS, 128), BF16), jax.ShapeDtypeStruct((2, 16), F32)),
        in_specs=[hbm] * 4,
        out_specs=(vmem, vmem),
        scratch_shapes=[
            pltpu.VMEM((4, 8, ROWS, 3600), BF16),
            pltpu.VMEM((900, 3600), BF16),
            pltpu.VMEM((1800, 375), BF16),
            pltpu.VMEM((16, 128), BF16),
            pltpu.VMEM((16, 128), F32),
            pltpu.VMEM((8, WIDE, 375), BF16),
            pltpu.VMEM((2, 8, ROWS, WIDE), F32),
            pltpu.VMEM((256, 128), BF16),
            pltpu.VMEM((4, NY - 1, 128, WIDE), BF16),
            pltpu.VMEM((4, 128, WIDE), F32),
            pltpu.VMEM((4, NY - 1, 128, WIDE), BF16),
            pltpu.VMEM((4, 8, ROWS, WIDE), BF16),
            pltpu.VMEM((4, 2, 8, ROWS, WIDE), BF16),
            pltpu.VMEM((4, NY, 8, ROWS, WIDE), BF16),
            pltpu.VMEM((375, 256), F32),
            pltpu.VMEM((2, 16, 128), F32),
            pltpu.VMEM((2, 128), F32),
            pltpu.VMEM((32, 2, 128), F32),
            dma((3,)),
            dma,
            dma((2, 4, 8)),
            dma((4, NY - 1)),
            dma((4,)),
            dma((4, NY - 1)),
            dma,
            pltpu.SemaphoreType.REGULAR((4,)),
            dma,
            dma,
            dma,
            dma,
            dma,
            dma,
        ],
        compiler_params=pltpu.CompilerParams(collective_id=0, has_side_effects=True, vmem_limit_bytes=58 * 2**20),
        cost_estimate=pl.CostEstimate(flops=5 * 10**9, bytes_accessed=12 * 2**20, transcendentals=0),
    )(density.T, cholesky, virtual_orbitals.T, occupied_orbitals.T)
    return back.transpose(1, 2, 0), lagrangian.T


def solution(mesh):
    return jax.shard_map(
        on_device,
        mesh=mesh,
        in_specs=(P("aux", "pair"), P("pair", "aux"), P("aux", None), P()),
        out_specs=(P("pair", None, "aux"), P(None, "aux")),
        check_vma=False,
    )
```

```python
import jax
import jax.numpy as jnp
from jax import lax
from jax.experimental import pallas as pl
from jax.experimental.pallas import tpu as pltpu
from jax.sharding import PartitionSpec as P

MESH = pl.DeviceIdType.MESH
F32 = jnp.float32
BF16 = jnp.bfloat16
NT = (((1,), (1,)), ((), ()))

NX, NY, NZ, NC = 4, 4, 4, 2
ROWS = 16
CUT = 224
LAST = 228
WIDE = 256
HALVES = (0, 1792, 3600)
NCHOL = 512


def kernel(
    dt_hbm, chol_hbm, virt_hbm, occ_hbm, turned, weights, lag_ref,
    gath, dt, virt, occ, occ32, virtp, lc, part, mine, fromy, summed, owned, gamma, lagrow, lagmine, lagall,
    local_sem, bulk_sem, block_sem, y_sem, own_sem, g_sem, lag_sem, plane_sem,
    send_first, send_second, send_y, send_own, send_g, send_lag,
):
    aux, pair = lax.axis_index("aux"), lax.axis_index("pair")
    zh, y = aux // NY, aux % NY
    x, zl, c = pair // (NZ * NC), (pair // NC) % NZ, pair % NC
    me = c * NX + x
    rows_of = (zl, zl + 1 - 2 * lax.rem(zl, 2), lax.rem(zl + 2, NZ), NZ - 1 - zl)

    auxes = [[(zh * NY if d == 0 else (1 - zh) * NY) + lax.rem(y + e, NY) for e in range(NY)] for d in range(2)]
    xs = [lax.rem(x + d, NX) for d in range(NX)]
    zs = [lax.rem(zl + d, NZ) for d in range(NZ)]
    cs = [c, 1 - c]

    def device(dzh=0, dy=0, dx=0, dz=0, dc=0):
        return (auxes[dzh][dy], (xs[dx] * NZ + zs[dz]) * NC + cs[dc])

    right, left, sibling, up, down = device(dx=1), device(dx=3), device(dc=1), device(dz=1), device(dz=3)
    across = device(dzh=1)

    barrier = pltpu.get_barrier_semaphore()
    friends = [right, left, sibling, up, down, across] + [device(dy=e) for e in range(1, NY)]
    for friend in friends:
        pl.semaphore_signal(barrier, inc=1, device_id=friend, device_id_type=MESH)

    own = pltpu.make_async_copy(chol_hbm, gath.at[0, c * NX], local_sem.at[0])
    own.start()
    load_occ = pltpu.make_async_copy(occ_hbm, occ, local_sem.at[2])
    load_occ.start()
    load_virt = pltpu.make_async_copy(virt_hbm, virt, local_sem.at[1])
    load_virt.start()
    load_dt = pltpu.make_async_copy(dt_hbm, dt, bulk_sem)
    load_dt.start()

    def block(src, dst, h, target):
        cols = pl.ds(HALVES[h], HALVES[h + 1] - HALVES[h])
        return pltpu.make_async_remote_copy(
            src_ref=gath.at[src[0], src[1], :, cols], dst_ref=gath.at[dst[0], dst[1], :, cols],
            send_sem=(send_first, send_second)[h], recv_sem=block_sem.at[h, dst[0], dst[1]],
            device_id=target, device_id_type=MESH,
        )

    def arrived(q, j, h):
        block((q, j), (q, j), h, sibling).wait_recv()

    def xor(a, b):
        return a + b - 2 * (lax.rem(a, 2) * lax.rem(b, 2)) - 4 * ((a // 2) * (b // 2))

    mine_first = c * NX

    def along_z(s_, h):
        above, below = zl + s_, zl - s_

        @pl.when(above < NZ)
        def _():
            at = xor(zl, above)
            if s_ > 0:
                arrived(at, mine_first, h)

            @pl.when(zl > 0)
            def _():
                block((at, mine_first), (xor(zl - 1, above), mine_first), h, down).start()

        @pl.when(below >= 0)
        def _():
            at = xor(zl, below)
            if s_ > 0:
                arrived(at, mine_first, h)

            @pl.when(zl < NZ - 1)
            def _():
                block((at, mine_first), (xor(zl + 1, below), mine_first), h, up).start()

    def own_column(q, h):
        along_z(q, h)
        block((q, mine_first), (q, mine_first + 3), h, right).start()
        block((q, mine_first), (q, mine_first + 1), h, left).start()
        block((q, mine_first), (q, mine_first), h, sibling).start()

    def beside(q, h):
        for g, other, target in ((1, 0, left), (3, 1, right)):
            j = mine_first + g
            arrived(q, j, h)
            if q % 2 == 1 - other:
                block((q, j), (q, mine_first + 2), h, target).start()
            block((q, j), (q, j), h, sibling).start()

    def opposite(q):
        j = mine_first + 2
        for h in range(2):
            arrived(q, j, h)
            block((q, j), (q, j), h, sibling).start()

    def from_sibling(q):
        for g in range(NX):
            for h in range(2):
                arrived(q, (1 - c) * NX + g, h)
        pl.semaphore_signal(plane_sem.at[q], inc=1, device_id=across, device_id_type=MESH)

    def over_y(k, t):
        return pltpu.make_async_remote_copy(
            src_ref=part.at[k, t], dst_ref=fromy.at[k, t], send_sem=send_y, recv_sem=y_sem.at[k, t],
            device_id=device(dy=t + 1), device_id_type=MESH,
        )

    def product(k, t):
        rows = gath[k].reshape(128, 3600)
        cut = lax.rem(y + 1 + t, NY)
        pairs = dt[pl.ds(pl.multiple_of(cut * CUT, 16), LAST), :]
        value = lax.dot_general(rows, pairs, NT, preferred_element_type=F32)
        if t < NY - 1:
            part[k, t, :, 0:LAST] = value.astype(BF16)
            over_y(k, t).start()
        else:
            mine[k, :, 0:LAST] = value

    def to_owner(k, dzh, g, dc):
        return pltpu.make_async_remote_copy(
            src_ref=summed.at[k, cs[dc] * NX + g], dst_ref=owned.at[k, zh, me],
            send_sem=send_own, recv_sem=own_sem.at[k],
            device_id=(auxes[dzh][0], (xs[g] * NZ + rows_of[k]) * NC + cs[dc]), device_id_type=MESH,
        )

    def sum_y(k):
        total = mine[k]
        for t in range(NY - 1):
            over_y(k, t).wait_recv()
            total = total + fromy[k, t].astype(F32)
        summed[k] = total.astype(BF16).reshape(8, ROWS, WIDE)
        pl.semaphore_wait(plane_sem.at[k], 1)
        for dzh in (1, 0):
            for g in (2, 1, 3, 0):
                for dc in range(NC):
                    if k == 0 and g == 0 and dc == 0 and dzh == 0:
                        pltpu.make_async_copy(summed.at[k, c * NX], owned.at[0, zh, me], own_sem.at[0]).start()
                    else:
                        to_owner(k, dzh, g, dc).start()

    def gather_y(k, t):
        return pltpu.make_async_remote_copy(
            src_ref=gamma.at[k, y], dst_ref=gamma.at[k, y], send_sem=send_g, recv_sem=g_sem.at[k, t],
            device_id=device(dy=t + 1), device_id_type=MESH,
        )

    def complete(k):
        pltpu.make_async_copy(owned.at[k], owned.at[k], own_sem.at[k]).wait()
        gamma[k, y] = (owned[k, 0].astype(F32) + owned[k, 1].astype(F32)).astype(BF16)
        for t in range(NY - 1):
            gather_y(k, t).start()

    def here(k):
        for t in range(NY - 1):
            gather_y(k, t).wait_recv()

    def half_done(k):
        total = jnp.zeros((64, 375), F32)
        for h in range(2):
            for cut in range(NY):
                total = total + jnp.dot(
                    gamma[k, cut, pl.ds(4 * h, 4)].reshape(64, WIDE), virtp[4 * h + cut], preferred_element_type=F32
                )
        turned[:, k * 64 : (k + 1) * 64] = total.astype(BF16).astype(F32).T

    def lagrangian(k):
        for z in range(NZ):
            i = z * NZ + rows_of[k]
            for j in range(2):
                terms = jnp.zeros((ROWS, WIDE), F32)
                for h in range(2):
                    for cut in range(NY):
                        terms = terms + gamma[k, cut, 4 * h + z].astype(F32) * lc[j, 4 * h + cut]
                terms = terms[:, :128] + terms[:, 128:]
                lagrow[j, pl.ds(i, 1), :] = jnp.sum(terms, axis=0, keepdims=True)

    def pad_virtual(h):
        for cut in range(NY):
            width = LAST if cut == NY - 1 else CUT
            start = h * 900 + cut * CUT
            first = start // 8 * 8
            value = virt[first : start + width, :].astype(F32)
            virtp[4 * h + cut, 0:width, :] = value[start - first :].astype(BF16)

    own.wait()
    virtp[...] = jnp.zeros(virtp.shape, BF16)
    pl.semaphore_wait(barrier, len(friends))
    own_column(0, 0)
    own_column(0, 1)

    own_column(1, 0)
    beside(0, 0)
    part[:, :, :, 128:WIDE] = jnp.zeros((4, NY - 1, 128, WIDE - 128), BF16)
    mine[:, :, 128:WIDE] = jnp.zeros((4, 128, WIDE - 128), F32)
    own_column(1, 1)
    beside(0, 1)
    lc[...] = jnp.zeros(lc.shape, F32)
    lagmine[...] = jnp.zeros(lagmine.shape, F32)
    load_occ.wait()
    occ32[...] = occ[...].astype(F32)
    for k in range(4):
        for z in range(NZ):
            row = occ32[pl.ds(z * NZ + rows_of[k], 1), :]
            weights[pl.ds(k * 64 + z * 16, 16), :] = jnp.broadcast_to(row, (16, 128)).astype(BF16)
    own_column(2, 0)
    load_virt.wait()
    pad_virtual(0)
    own_column(2, 1)
    opposite(0)
    beside(1, 0)
    pad_virtual(1)
    beside(1, 1)
    own_column(3, 0)
    own_column(3, 1)
    own_block = gath[0, c * NX].astype(F32)
    for j in range(2):
        for h in range(2):
            for cut in range(NY):
                width = LAST if cut == NY - 1 else CUT
                start = j * 1800 + h * 900 + cut * CUT
                lc[j, 4 * h + cut, :, 0:width] = own_block[:, start : start + width]
    from_sibling(0)
    load_dt.wait()
    product(0, 0)
    beside(2, 0)
    product(0, 1)
    beside(2, 1)
    product(0, 2)
    opposite(1)
    product(0, 3)
    beside(3, 0)
    from_sibling(1)
    product(1, 0)
    beside(3, 1)
    product(1, 1)
    product(1, 2)
    opposite(2)
    product(1, 3)
    sum_y(0)
    from_sibling(2)
    product(2, 0)
    product(2, 1)
    opposite(3)
    product(2, 2)
    product(2, 3)
    sum_y(1)
    from_sibling(3)
    for t in range(NY):
        product(3, t)
    sum_y(2)
    complete(0)
    sum_y(3)
    complete(1)
    complete(2)
    complete(3)
    for k in range(3):
        here(k)
        lagrangian(k)
    half_done(0)
    here(3)
    lagrangian(3)

    lagmine[0:2, 0:16] = jnp.sum(lagrow[...], axis=-1) * (1.0 / NCHOL)

    def share(t):
        return pltpu.make_async_remote_copy(
            src_ref=lagmine, dst_ref=lagall.at[pair], send_sem=send_lag, recv_sem=lag_sem,
            device_id=(aux, lax.rem(pair + t, 32)), device_id_type=MESH,
        )

    def start_share(t, carry):
        share(t).start()
        return carry

    pltpu.make_async_copy(lagmine, lagall.at[pair], lag_sem).start()
    lax.fori_loop(1, 32, start_share, 0)

    for k in range(1, 4):
        half_done(k)
    pltpu.make_async_copy(lagall, lagall, lag_sem).wait()
    lag_ref[...] = jnp.sum(lagall[...], axis=0)[0:2, 0:16]

    sent = 28 + jnp.where(zl < NZ - 1, zl + 1, 0) + jnp.where(zl > 0, NZ - zl, 0)

    def left_block(t, carry):
        block((0, 0), (0, 0), 0, sibling).wait_send()
        block((0, 0), (0, 0), 1, sibling).wait_send()
        return carry

    def left_y(t, carry):
        over_y(0, 0).wait_send()
        gather_y(0, 0).wait_send()
        return carry

    def left_own(t, carry):
        to_owner(1, 0, 0, 0).wait_send()
        return carry

    def left_lag(t, carry):
        share(1).wait_send()
        return carry

    lax.fori_loop(0, sent, left_block, 0)
    lax.fori_loop(0, 12, left_y, 0)
    lax.fori_loop(0, 63, left_own, 0)
    lax.fori_loop(0, 31, left_lag, 0)


def second(turned, weights, terms, out_hbm, lag_ref, out, sem):
    row = lax.broadcasted_iota(jnp.int32, (ROWS, 256), 0)
    lane = lax.broadcasted_iota(jnp.int32, (ROWS, 256), 1)
    keep = (lane % ROWS) == row
    copies = []
    for start in range(0, 375, 64):
        n = min(64, 375 - start)
        spread = jnp.where(keep[None], turned[start : start + n][:, None, :], 0.0).astype(BF16)
        value = jnp.dot(spread.reshape(n * ROWS, 256), weights[...], preferred_element_type=F32)
        out[start : start + n] = value.astype(BF16).reshape(n, ROWS, 128)
        rows = pl.ds(start, n)
        copies.append(pltpu.make_async_copy(out.at[rows], out_hbm.at[rows], sem.at[start // 64]))
        copies[-1].start()
    lag_ref[...] = terms[...]
    for copy in copies:
        copy.wait()


def on_device(density, cholesky, virtual_orbitals, occupied_orbitals):
    hbm = pl.BlockSpec(memory_space=pltpu.HBM)
    vmem = pl.BlockSpec(memory_space=pltpu.VMEM)
    dma = pltpu.SemaphoreType.DMA
    turned, weights, terms = pl.pallas_call(
        kernel,
        name="density",
        out_shape=(
            jax.ShapeDtypeStruct((375, 256), F32),
            jax.ShapeDtypeStruct((256, 128), BF16),
            jax.ShapeDtypeStruct((2, 16), F32),
        ),
        in_specs=[hbm] * 4,
        out_specs=(vmem, vmem, vmem),
        scratch_shapes=[
            pltpu.VMEM((4, 8, ROWS, 3600), BF16),
            pltpu.VMEM((900, 3600), BF16),
            pltpu.VMEM((1800, 375), BF16),
            pltpu.VMEM((16, 128), BF16),
            pltpu.VMEM((16, 128), F32),
            pltpu.VMEM((8, WIDE, 375), BF16),
            pltpu.VMEM((2, 8, ROWS, WIDE), F32),
            pltpu.VMEM((4, NY - 1, 128, WIDE), BF16),
            pltpu.VMEM((4, 128, WIDE), F32),
            pltpu.VMEM((4, NY - 1, 128, WIDE), BF16),
            pltpu.VMEM((4, 8, ROWS, WIDE), BF16),
            pltpu.VMEM((4, 2, 8, ROWS, WIDE), BF16),
            pltpu.VMEM((4, NY, 8, ROWS, WIDE), BF16),
            pltpu.VMEM((2, 16, 128), F32),
            pltpu.VMEM((2, 128), F32),
            pltpu.VMEM((32, 2, 128), F32),
            dma((3,)),
            dma,
            dma((2, 4, 8)),
            dma((4, NY - 1)),
            dma((4,)),
            dma((4, NY - 1)),
            dma,
            pltpu.SemaphoreType.REGULAR((4,)),
            dma,
            dma,
            dma,
            dma,
            dma,
            dma,
        ],
        compiler_params=pltpu.CompilerParams(collective_id=0, has_side_effects=True, vmem_limit_bytes=58 * 2**20),
        cost_estimate=pl.CostEstimate(flops=5 * 10**9, bytes_accessed=12 * 2**20, transcendentals=0),
    )(density.T, cholesky, virtual_orbitals.T, occupied_orbitals.T)
    back, lagrangian = pl.pallas_call(
        second,
        name="second",
        out_shape=(jax.ShapeDtypeStruct((375, ROWS, 128), BF16), jax.ShapeDtypeStruct((2, 16), F32)),
        in_specs=[vmem] * 3,
        out_specs=(hbm, vmem),
        scratch_shapes=[pltpu.VMEM((375, ROWS, 128), BF16), dma((6,))],
        compiler_params=pltpu.CompilerParams(vmem_limit_bytes=60 * 2**20),
        cost_estimate=pl.CostEstimate(flops=4 * 10**8, bytes_accessed=2 * 2**20, transcendentals=0),
    )(turned, weights, terms)
    return back.transpose(1, 2, 0), lagrangian.T


def solution(mesh):
    return jax.shard_map(
        on_device,
        mesh=mesh,
        in_specs=(P("aux", "pair"), P("pair", "aux"), P("aux", None), P()),
        out_specs=(P("pair", None, "aux"), P(None, "aux")),
        check_vma=False,
    )
```

```python
import jax
import jax.numpy as jnp
from jax import lax
from jax.experimental import pallas as pl
from jax.experimental.pallas import tpu as pltpu
from jax.sharding import PartitionSpec as P

MESH = pl.DeviceIdType.MESH
F32 = jnp.float32
BF16 = jnp.bfloat16
NT = (((1,), (1,)), ((), ()))

NX, NY, NZ, NC = 4, 4, 4, 2
ROWS = 16
CUT = 224
LAST = 228
WIDE = 256
HALVES = (0, 1792, 3600)
NCHOL = 512


def kernel(
    dt_hbm, chol_hbm, virt_hbm, occ_hbm, turned, weights, lag_ref,
    gath, dt, virt, occ, occ32, virtp, lc, part, mine, fromy, summed, owned, gamma, lagrow, lagmine, lagall,
    local_sem, bulk_sem, block_sem, y_sem, own_sem, g_sem, lag_sem, plane_sem,
    send_first, send_second, send_y, send_own, send_g, send_lag,
):
    aux, pair = lax.axis_index("aux"), lax.axis_index("pair")
    zh, y = aux // NY, aux % NY
    x, zl, c = pair // (NZ * NC), (pair // NC) % NZ, pair % NC
    me = c * NX + x
    rows_of = (zl, zl + 1 - 2 * lax.rem(zl, 2), lax.rem(zl + 2, NZ), NZ - 1 - zl)

    auxes = [[(zh * NY if d == 0 else (1 - zh) * NY) + lax.rem(y + e, NY) for e in range(NY)] for d in range(2)]
    xs = [lax.rem(x + d, NX) for d in range(NX)]
    zs = [lax.rem(zl + d, NZ) for d in range(NZ)]
    cs = [c, 1 - c]

    def device(dzh=0, dy=0, dx=0, dz=0, dc=0):
        return (auxes[dzh][dy], (xs[dx] * NZ + zs[dz]) * NC + cs[dc])

    right, left, sibling, up, down = device(dx=1), device(dx=3), device(dc=1), device(dz=1), device(dz=3)
    across = device(dzh=1)

    barrier = pltpu.get_barrier_semaphore()
    friends = [right, left, sibling, up, down, across] + [device(dy=e) for e in range(1, NY)]
    for friend in friends:
        pl.semaphore_signal(barrier, inc=1, device_id=friend, device_id_type=MESH)

    own = pltpu.make_async_copy(chol_hbm, gath.at[0, c * NX], local_sem.at[0])
    own.start()
    load_occ = pltpu.make_async_copy(occ_hbm, occ, local_sem.at[2])
    load_occ.start()
    load_virt = pltpu.make_async_copy(virt_hbm, virt, local_sem.at[1])
    load_virt.start()
    load_dt = pltpu.make_async_copy(dt_hbm, dt, bulk_sem)
    load_dt.start()

    def block(src, dst, h, target):
        cols = pl.ds(HALVES[h], HALVES[h + 1] - HALVES[h])
        return pltpu.make_async_remote_copy(
            src_ref=gath.at[src[0], src[1], :, cols], dst_ref=gath.at[dst[0], dst[1], :, cols],
            send_sem=(send_first, send_second)[h], recv_sem=block_sem.at[h, dst[0], dst[1]],
            device_id=target, device_id_type=MESH,
        )

    def arrived(q, j, h):
        block((q, j), (q, j), h, sibling).wait_recv()

    def xor(a, b):
        return a + b - 2 * (lax.rem(a, 2) * lax.rem(b, 2)) - 4 * ((a // 2) * (b // 2))

    mine_first = c * NX

    def along_z(s_, h):
        above, below = zl + s_, zl - s_

        @pl.when(above < NZ)
        def _():
            at = xor(zl, above)
            if s_ > 0:
                arrived(at, mine_first, h)

            @pl.when(zl > 0)
            def _():
                block((at, mine_first), (xor(zl - 1, above), mine_first), h, down).start()

        @pl.when(below >= 0)
        def _():
            at = xor(zl, below)
            if s_ > 0:
                arrived(at, mine_first, h)

            @pl.when(zl < NZ - 1)
            def _():
                block((at, mine_first), (xor(zl + 1, below), mine_first), h, up).start()

    def own_column(q, h):
        along_z(q, h)
        block((q, mine_first), (q, mine_first + 3), h, right).start()
        block((q, mine_first), (q, mine_first + 1), h, left).start()
        block((q, mine_first), (q, mine_first), h, sibling).start()

    def beside(q, h):
        for g, other, target in ((1, 0, left), (3, 1, right)):
            j = mine_first + g
            arrived(q, j, h)
            if q % 2 == 1 - other:
                block((q, j), (q, mine_first + 2), h, target).start()
            block((q, j), (q, j), h, sibling).start()

    def opposite(q):
        j = mine_first + 2
        for h in range(2):
            arrived(q, j, h)
            block((q, j), (q, j), h, sibling).start()

    def from_sibling(q):
        for g in range(NX):
            for h in range(2):
                arrived(q, (1 - c) * NX + g, h)
        pl.semaphore_signal(plane_sem.at[q], inc=1, device_id=across, device_id_type=MESH)

    def over_y(k, t):
        return pltpu.make_async_remote_copy(
            src_ref=part.at[k, t], dst_ref=fromy.at[k, t], send_sem=send_y, recv_sem=y_sem.at[k, t],
            device_id=device(dy=t + 1), device_id_type=MESH,
        )

    def product(k, t):
        rows = gath[k].reshape(128, 3600)
        cut = lax.rem(y + 1 + t, NY)
        pairs = dt[pl.ds(pl.multiple_of(cut * CUT, 16), LAST), :]
        value = lax.dot_general(rows, pairs, NT, preferred_element_type=F32)
        if t < NY - 1:
            part[k, t, :, 0:LAST] = value.astype(BF16)
            over_y(k, t).start()
        else:
            mine[k, :, 0:LAST] = value

    def to_owner(k, dzh, g, dc):
        return pltpu.make_async_remote_copy(
            src_ref=summed.at[k, cs[dc] * NX + g], dst_ref=owned.at[k, zh, me],
            send_sem=send_own, recv_sem=own_sem.at[k],
            device_id=(auxes[dzh][0], (xs[g] * NZ + rows_of[k]) * NC + cs[dc]), device_id_type=MESH,
        )

    def sum_y(k):
        total = mine[k]
        for t in range(NY - 1):
            over_y(k, t).wait_recv()
            total = total + fromy[k, t].astype(F32)
        summed[k] = total.astype(BF16).reshape(8, ROWS, WIDE)
        pl.semaphore_wait(plane_sem.at[k], 1)
        for dzh in (1, 0):
            for g in (2, 1, 3, 0):
                for dc in range(NC):
                    if k == 0 and g == 0 and dc == 0 and dzh == 0:
                        pltpu.make_async_copy(summed.at[k, c * NX], owned.at[0, zh, me], own_sem.at[0]).start()
                    else:
                        to_owner(k, dzh, g, dc).start()

    def gather_y(k, t):
        return pltpu.make_async_remote_copy(
            src_ref=gamma.at[k, y], dst_ref=gamma.at[k, y], send_sem=send_g, recv_sem=g_sem.at[k, t],
            device_id=device(dy=t + 1), device_id_type=MESH,
        )

    def complete(k):
        pltpu.make_async_copy(owned.at[k], owned.at[k], own_sem.at[k]).wait()
        gamma[k, y] = (owned[k, 0].astype(F32) + owned[k, 1].astype(F32)).astype(BF16)
        for t in range(NY - 1):
            gather_y(k, t).start()

    def here(k):
        for t in range(NY - 1):
            gather_y(k, t).wait_recv()

    def half_done(k):
        total = jnp.zeros((64, 375), F32)
        for h in range(2):
            for cut in range(NY):
                total = total + jnp.dot(
                    gamma[k, cut, pl.ds(4 * h, 4)].reshape(64, WIDE), virtp[4 * h + cut], preferred_element_type=F32
                )
        turned[:, k * 64 : (k + 1) * 64] = total.astype(BF16).astype(F32).T

    def lagrangian(k):
        for z in range(NZ):
            i = z * NZ + rows_of[k]
            for j in range(2):
                terms = jnp.zeros((ROWS, WIDE), F32)
                for h in range(2):
                    for cut in range(NY):
                        terms = terms + gamma[k, cut, 4 * h + z].astype(F32) * lc[j, 4 * h + cut]
                terms = terms[:, :128] + terms[:, 128:]
                lagrow[j, pl.ds(i, 1), :] = jnp.sum(terms, axis=0, keepdims=True)

    def pad_virtual(h):
        for cut in range(NY):
            width = LAST if cut == NY - 1 else CUT
            start = h * 900 + cut * CUT
            first = start // 8 * 8
            value = virt[first : start + width, :].astype(F32)
            virtp[4 * h + cut, 0:width, :] = value[start - first :].astype(BF16)

    own.wait()
    virtp[...] = jnp.zeros(virtp.shape, BF16)
    pl.semaphore_wait(barrier, len(friends))
    own_column(0, 0)
    own_column(0, 1)

    own_column(1, 0)
    beside(0, 0)
    part[:, :, :, 128:WIDE] = jnp.zeros((4, NY - 1, 128, WIDE - 128), BF16)
    mine[:, :, 128:WIDE] = jnp.zeros((4, 128, WIDE - 128), F32)
    own_column(1, 1)
    beside(0, 1)
    lc[...] = jnp.zeros(lc.shape, F32)
    lagmine[...] = jnp.zeros(lagmine.shape, F32)
    load_occ.wait()
    occ32[...] = occ[...].astype(F32)
    for k in range(4):
        for z in range(NZ):
            row = occ32[pl.ds(z * NZ + rows_of[k], 1), :]
            weights[pl.ds(k * 64 + z * 16, 16), :] = jnp.broadcast_to(row, (16, 128)).astype(BF16)
    own_column(2, 0)
    load_virt.wait()
    pad_virtual(0)
    own_column(2, 1)
    opposite(0)
    beside(1, 0)
    pad_virtual(1)
    beside(1, 1)
    own_column(3, 0)
    own_column(3, 1)
    own_block = gath[0, c * NX].astype(F32)
    for j in range(2):
        for h in range(2):
            for cut in range(NY):
                width = LAST if cut == NY - 1 else CUT
                start = j * 1800 + h * 900 + cut * CUT
                lc[j, 4 * h + cut, :, 0:width] = own_block[:, start : start + width]
    from_sibling(0)
    load_dt.wait()
    product(0, 0)
    beside(2, 0)
    product(0, 1)
    beside(2, 1)
    product(0, 2)
    opposite(1)
    product(0, 3)
    beside(3, 0)
    from_sibling(1)
    product(1, 0)
    beside(3, 1)
    product(1, 1)
    product(1, 2)
    opposite(2)
    product(1, 3)
    sum_y(0)
    from_sibling(2)
    product(2, 0)
    product(2, 1)
    opposite(3)
    product(2, 2)
    product(2, 3)
    sum_y(1)
    from_sibling(3)
    product(3, 0)
    product(3, 1)
    sum_y(2)
    product(3, 2)
    product(3, 3)
    complete(0)
    sum_y(3)
    complete(1)
    complete(2)
    complete(3)
    for k in range(3):
        here(k)
        lagrangian(k)
    half_done(0)
    here(3)
    lagrangian(3)

    lagmine[0:2, 0:16] = jnp.sum(lagrow[...], axis=-1) * (1.0 / NCHOL)

    def share(t):
        return pltpu.make_async_remote_copy(
            src_ref=lagmine, dst_ref=lagall.at[pair], send_sem=send_lag, recv_sem=lag_sem,
            device_id=(aux, lax.rem(pair + t, 32)), device_id_type=MESH,
        )

    def start_share(t, carry):
        share(t).start()
        return carry

    pltpu.make_async_copy(lagmine, lagall.at[pair], lag_sem).start()
    lax.fori_loop(1, 32, start_share, 0)

    for k in range(1, 4):
        half_done(k)
    pltpu.make_async_copy(lagall, lagall, lag_sem).wait()
    lag_ref[...] = jnp.sum(lagall[...], axis=0)[0:2, 0:16]

    sent = 28 + jnp.where(zl < NZ - 1, zl + 1, 0) + jnp.where(zl > 0, NZ - zl, 0)

    def left_block(t, carry):
        block((0, 0), (0, 0), 0, sibling).wait_send()
        block((0, 0), (0, 0), 1, sibling).wait_send()
        return carry

    def left_y(t, carry):
        over_y(0, 0).wait_send()
        gather_y(0, 0).wait_send()
        return carry

    def left_own(t, carry):
        to_owner(1, 0, 0, 0).wait_send()
        return carry

    def left_lag(t, carry):
        share(1).wait_send()
        return carry

    lax.fori_loop(0, sent, left_block, 0)
    lax.fori_loop(0, 12, left_y, 0)
    lax.fori_loop(0, 63, left_own, 0)
    lax.fori_loop(0, 31, left_lag, 0)


def second(turned, weights, terms, out_hbm, lag_ref, out, sem):
    row = lax.broadcasted_iota(jnp.int32, (ROWS, 256), 0)
    lane = lax.broadcasted_iota(jnp.int32, (ROWS, 256), 1)
    keep = (lane % ROWS) == row
    copies = []
    for start in range(0, 375, 64):
        n = min(64, 375 - start)
        spread = jnp.where(keep[None], turned[start : start + n][:, None, :], 0.0).astype(BF16)
        value = jnp.dot(spread.reshape(n * ROWS, 256), weights[...], preferred_element_type=F32)
        out[start : start + n] = value.astype(BF16).reshape(n, ROWS, 128)
        rows = pl.ds(start, n)
        copies.append(pltpu.make_async_copy(out.at[rows], out_hbm.at[rows], sem.at[start // 64]))
        copies[-1].start()
    lag_ref[...] = terms[...]
    for copy in copies:
        copy.wait()


def on_device(density, cholesky, virtual_orbitals, occupied_orbitals):
    hbm = pl.BlockSpec(memory_space=pltpu.HBM)
    vmem = pl.BlockSpec(memory_space=pltpu.VMEM)
    dma = pltpu.SemaphoreType.DMA
    turned, weights, terms = pl.pallas_call(
        kernel,
        name="density",
        out_shape=(
            jax.ShapeDtypeStruct((375, 256), F32),
            jax.ShapeDtypeStruct((256, 128), BF16),
            jax.ShapeDtypeStruct((2, 16), F32),
        ),
        in_specs=[hbm] * 4,
        out_specs=(vmem, vmem, vmem),
        scratch_shapes=[
            pltpu.VMEM((4, 8, ROWS, 3600), BF16),
            pltpu.VMEM((900, 3600), BF16),
            pltpu.VMEM((1800, 375), BF16),
            pltpu.VMEM((16, 128), BF16),
            pltpu.VMEM((16, 128), F32),
            pltpu.VMEM((8, WIDE, 375), BF16),
            pltpu.VMEM((2, 8, ROWS, WIDE), F32),
            pltpu.VMEM((4, NY - 1, 128, WIDE), BF16),
            pltpu.VMEM((4, 128, WIDE), F32),
            pltpu.VMEM((4, NY - 1, 128, WIDE), BF16),
            pltpu.VMEM((4, 8, ROWS, WIDE), BF16),
            pltpu.VMEM((4, 2, 8, ROWS, WIDE), BF16),
            pltpu.VMEM((4, NY, 8, ROWS, WIDE), BF16),
            pltpu.VMEM((2, 16, 128), F32),
            pltpu.VMEM((2, 128), F32),
            pltpu.VMEM((32, 2, 128), F32),
            dma((3,)),
            dma,
            dma((2, 4, 8)),
            dma((4, NY - 1)),
            dma((4,)),
            dma((4, NY - 1)),
            dma,
            pltpu.SemaphoreType.REGULAR((4,)),
            dma,
            dma,
            dma,
            dma,
            dma,
            dma,
        ],
        compiler_params=pltpu.CompilerParams(collective_id=0, has_side_effects=True, vmem_limit_bytes=58 * 2**20),
        cost_estimate=pl.CostEstimate(flops=5 * 10**9, bytes_accessed=12 * 2**20, transcendentals=0),
    )(density.T, cholesky, virtual_orbitals.T, occupied_orbitals.T)
    back, lagrangian = pl.pallas_call(
        second,
        name="second",
        out_shape=(jax.ShapeDtypeStruct((375, ROWS, 128), BF16), jax.ShapeDtypeStruct((2, 16), F32)),
        in_specs=[vmem] * 3,
        out_specs=(hbm, vmem),
        scratch_shapes=[pltpu.VMEM((375, ROWS, 128), BF16), dma((6,))],
        compiler_params=pltpu.CompilerParams(vmem_limit_bytes=60 * 2**20),
        cost_estimate=pl.CostEstimate(flops=4 * 10**8, bytes_accessed=2 * 2**20, transcendentals=0),
    )(turned, weights, terms)
    return back.transpose(1, 2, 0), lagrangian.T


def solution(mesh):
    return jax.shard_map(
        on_device,
        mesh=mesh,
        in_specs=(P("aux", "pair"), P("pair", "aux"), P("aux", None), P()),
        out_specs=(P("pair", None, "aux"), P(None, "aux")),
        check_vma=False,
    )
```

```python
import jax
import jax.numpy as jnp
from jax import lax
from jax.experimental import pallas as pl
from jax.experimental.pallas import tpu as pltpu
from jax.sharding import PartitionSpec as P

MESH = pl.DeviceIdType.MESH
F32 = jnp.float32
BF16 = jnp.bfloat16
NT = (((1,), (1,)), ((), ()))

NX, NY, NZ, NC = 4, 4, 4, 2
ROWS = 16
CUT = 224
LAST = 228
WIDE = 256
HALVES = (0, 1792, 3600)
NCHOL = 512


def kernel(
    dt_hbm, chol_hbm, virt_hbm, occ_hbm, turned, weights, lag_ref,
    gath, dt, virt, occ, occ32, virtp, lc, part, mine, fromy, summed, owned, gamma, lagrow, lagmine, lagall,
    local_sem, bulk_sem, block_sem, y_sem, own_sem, g_sem, lag_sem, plane_sem,
    send_first, send_second, send_y, send_own, send_g, send_lag,
):
    aux, pair = lax.axis_index("aux"), lax.axis_index("pair")
    zh, y = aux // NY, aux % NY
    x, zl, c = pair // (NZ * NC), (pair // NC) % NZ, pair % NC
    me = c * NX + x
    rows_of = (zl, zl + 1 - 2 * lax.rem(zl, 2), lax.rem(zl + 2, NZ), NZ - 1 - zl)

    auxes = [[(zh * NY if d == 0 else (1 - zh) * NY) + lax.rem(y + e, NY) for e in range(NY)] for d in range(2)]
    xs = [lax.rem(x + d, NX) for d in range(NX)]
    zs = [lax.rem(zl + d, NZ) for d in range(NZ)]
    cs = [c, 1 - c]

    def device(dzh=0, dy=0, dx=0, dz=0, dc=0):
        return (auxes[dzh][dy], (xs[dx] * NZ + zs[dz]) * NC + cs[dc])

    right, left, sibling, up, down = device(dx=1), device(dx=3), device(dc=1), device(dz=1), device(dz=3)
    across = device(dzh=1)

    barrier = pltpu.get_barrier_semaphore()
    friends = [right, left, sibling, up, down, across] + [device(dy=e) for e in range(1, NY)]
    for friend in friends:
        pl.semaphore_signal(barrier, inc=1, device_id=friend, device_id_type=MESH)

    own = pltpu.make_async_copy(chol_hbm, gath.at[0, c * NX], local_sem.at[0])
    own.start()
    load_occ = pltpu.make_async_copy(occ_hbm, occ, local_sem.at[2])
    load_occ.start()
    load_virt = pltpu.make_async_copy(virt_hbm, virt, local_sem.at[1])
    load_virt.start()
    load_dt = pltpu.make_async_copy(dt_hbm, dt, bulk_sem)
    load_dt.start()

    def block(src, dst, h, target):
        cols = pl.ds(HALVES[h], HALVES[h + 1] - HALVES[h])
        return pltpu.make_async_remote_copy(
            src_ref=gath.at[src[0], src[1], :, cols], dst_ref=gath.at[dst[0], dst[1], :, cols],
            send_sem=(send_first, send_second)[h], recv_sem=block_sem.at[h, dst[0], dst[1]],
            device_id=target, device_id_type=MESH,
        )

    def arrived(q, j, h):
        block((q, j), (q, j), h, sibling).wait_recv()

    def xor(a, b):
        return a + b - 2 * (lax.rem(a, 2) * lax.rem(b, 2)) - 4 * ((a // 2) * (b // 2))

    mine_first = c * NX

    def along_z(s_, h):
        above, below = zl + s_, zl - s_

        @pl.when(above < NZ)
        def _():
            at = xor(zl, above)
            if s_ > 0:
                arrived(at, mine_first, h)

            @pl.when(zl > 0)
            def _():
                block((at, mine_first), (xor(zl - 1, above), mine_first), h, down).start()

        @pl.when(below >= 0)
        def _():
            at = xor(zl, below)
            if s_ > 0:
                arrived(at, mine_first, h)

            @pl.when(zl < NZ - 1)
            def _():
                block((at, mine_first), (xor(zl + 1, below), mine_first), h, up).start()

    def own_column(q, h):
        along_z(q, h)
        block((q, mine_first), (q, mine_first + 3), h, right).start()
        block((q, mine_first), (q, mine_first + 1), h, left).start()
        block((q, mine_first), (q, mine_first), h, sibling).start()

    def beside(q, h):
        for g, other, target in ((1, 0, left), (3, 1, right)):
            j = mine_first + g
            arrived(q, j, h)
            if q % 2 == 1 - other:
                block((q, j), (q, mine_first + 2), h, target).start()
            block((q, j), (q, j), h, sibling).start()

    def opposite(q):
        j = mine_first + 2
        for h in range(2):
            arrived(q, j, h)
            block((q, j), (q, j), h, sibling).start()

    def from_sibling(q):
        for g in range(NX):
            for h in range(2):
                arrived(q, (1 - c) * NX + g, h)
        pl.semaphore_signal(plane_sem.at[q], inc=1, device_id=across, device_id_type=MESH)

    def over_y(k, t):
        return pltpu.make_async_remote_copy(
            src_ref=part.at[k, t], dst_ref=fromy.at[k, t], send_sem=send_y, recv_sem=y_sem.at[k, t],
            device_id=device(dy=t + 1), device_id_type=MESH,
        )

    def product(k, t):
        rows = gath[k].reshape(128, 3600)
        cut = lax.rem(y + 1 + t, NY)
        pairs = dt[pl.ds(pl.multiple_of(cut * CUT, 16), LAST), :]
        value = lax.dot_general(rows, pairs, NT, preferred_element_type=F32)
        if t < NY - 1:
            part[k, t, :, 0:LAST] = value.astype(BF16)
            over_y(k, t).start()
        else:
            mine[k, :, 0:LAST] = value

    def to_owner(k, dzh, g, dc):
        return pltpu.make_async_remote_copy(
            src_ref=summed.at[k, cs[dc] * NX + g], dst_ref=owned.at[k, zh, me],
            send_sem=send_own, recv_sem=own_sem.at[k],
            device_id=(auxes[dzh][0], (xs[g] * NZ + rows_of[k]) * NC + cs[dc]), device_id_type=MESH,
        )

    def sum_y(k):
        total = mine[k]
        for t in range(NY - 1):
            over_y(k, t).wait_recv()
            total = total + fromy[k, t].astype(F32)
        summed[k] = total.astype(BF16).reshape(8, ROWS, WIDE)
        pl.semaphore_wait(plane_sem.at[k], 1)
        for dzh in (1, 0):
            for g in (2, 1, 3, 0):
                for dc in range(NC):
                    if k == 0 and g == 0 and dc == 0 and dzh == 0:
                        pltpu.make_async_copy(summed.at[k, c * NX], owned.at[0, zh, me], own_sem.at[0]).start()
                    else:
                        to_owner(k, dzh, g, dc).start()

    def gather_y(k, t):
        return pltpu.make_async_remote_copy(
            src_ref=gamma.at[k, y], dst_ref=gamma.at[k, y], send_sem=send_g, recv_sem=g_sem.at[k, t],
            device_id=device(dy=t + 1), device_id_type=MESH,
        )

    def complete(k):
        pltpu.make_async_copy(owned.at[k], owned.at[k], own_sem.at[k]).wait()
        gamma[k, y] = (owned[k, 0].astype(F32) + owned[k, 1].astype(F32)).astype(BF16)
        for t in range(NY - 1):
            gather_y(k, t).start()

    def here(k):
        for t in range(NY - 1):
            gather_y(k, t).wait_recv()

    def half_done(k):
        total = jnp.zeros((64, 375), F32)
        for h in range(2):
            for cut in range(NY):
                total = total + jnp.dot(
                    gamma[k, cut, pl.ds(4 * h, 4)].reshape(64, WIDE), virtp[4 * h + cut], preferred_element_type=F32
                )
        turned[:, k * 64 : (k + 1) * 64] = total.T.astype(BF16)

    def lagrangian(k):
        for z in range(NZ):
            i = z * NZ + rows_of[k]
            for j in range(2):
                terms = jnp.zeros((ROWS, WIDE), F32)
                for h in range(2):
                    for cut in range(NY):
                        terms = terms + gamma[k, cut, 4 * h + z].astype(F32) * lc[j, 4 * h + cut]
                terms = terms[:, :128] + terms[:, 128:]
                lagrow[j, pl.ds(i, 1), :] = jnp.sum(terms, axis=0, keepdims=True)

    def pad_virtual(h):
        for cut in range(NY):
            width = LAST if cut == NY - 1 else CUT
            start = h * 900 + cut * CUT
            first = start // 8 * 8
            value = virt[first : start + width, :].astype(F32)
            virtp[4 * h + cut, 0:width, :] = value[start - first :].astype(BF16)

    own.wait()
    virtp[...] = jnp.zeros(virtp.shape, BF16)
    pl.semaphore_wait(barrier, len(friends))
    own_column(0, 0)
    own_column(0, 1)

    own_column(1, 0)
    beside(0, 0)
    part[:, :, :, 128:WIDE] = jnp.zeros((4, NY - 1, 128, WIDE - 128), BF16)
    mine[:, :, 128:WIDE] = jnp.zeros((4, 128, WIDE - 128), F32)
    own_column(1, 1)
    beside(0, 1)
    lc[...] = jnp.zeros(lc.shape, F32)
    lagmine[...] = jnp.zeros(lagmine.shape, F32)
    load_occ.wait()
    occ32[...] = occ[...].astype(F32)
    for k in range(4):
        for z in range(NZ):
            row = occ32[pl.ds(z * NZ + rows_of[k], 1), :]
            weights[pl.ds(k * 64 + z * 16, 16), :] = jnp.broadcast_to(row, (16, 128)).astype(BF16)
    own_column(2, 0)
    load_virt.wait()
    pad_virtual(0)
    own_column(2, 1)
    opposite(0)
    beside(1, 0)
    pad_virtual(1)
    beside(1, 1)
    own_column(3, 0)
    own_column(3, 1)
    own_block = gath[0, c * NX].astype(F32)
    for j in range(2):
        for h in range(2):
            for cut in range(NY):
                width = LAST if cut == NY - 1 else CUT
                start = j * 1800 + h * 900 + cut * CUT
                lc[j, 4 * h + cut, :, 0:width] = own_block[:, start : start + width]
    from_sibling(0)
    load_dt.wait()
    product(0, 0)
    beside(2, 0)
    product(0, 1)
    beside(2, 1)
    product(0, 2)
    opposite(1)
    product(0, 3)
    beside(3, 0)
    from_sibling(1)
    product(1, 0)
    beside(3, 1)
    product(1, 1)
    product(1, 2)
    opposite(2)
    product(1, 3)
    sum_y(0)
    from_sibling(2)
    product(2, 0)
    product(2, 1)
    opposite(3)
    product(2, 2)
    sum_y(1)
    product(2, 3)
    from_sibling(3)
    product(3, 0)
    product(3, 1)
    sum_y(2)
    product(3, 2)
    product(3, 3)
    complete(0)
    sum_y(3)
    complete(1)
    complete(2)
    complete(3)
    for k in range(3):
        here(k)
        lagrangian(k)
    half_done(0)
    here(3)
    lagrangian(3)

    lagmine[0:2, 0:16] = jnp.sum(lagrow[...], axis=-1) * (1.0 / NCHOL)

    def share(t):
        return pltpu.make_async_remote_copy(
            src_ref=lagmine, dst_ref=lagall.at[pair], send_sem=send_lag, recv_sem=lag_sem,
            device_id=(aux, lax.rem(pair + t, 32)), device_id_type=MESH,
        )

    def start_share(t, carry):
        share(t).start()
        return carry

    pltpu.make_async_copy(lagmine, lagall.at[pair], lag_sem).start()
    lax.fori_loop(1, 32, start_share, 0)

    for k in range(1, 4):
        half_done(k)
    pltpu.make_async_copy(lagall, lagall, lag_sem).wait()
    lag_ref[...] = jnp.sum(lagall[...], axis=0)[0:2, 0:16]

    sent = 28 + jnp.where(zl < NZ - 1, zl + 1, 0) + jnp.where(zl > 0, NZ - zl, 0)

    def left_block(t, carry):
        block((0, 0), (0, 0), 0, sibling).wait_send()
        block((0, 0), (0, 0), 1, sibling).wait_send()
        return carry

    def left_y(t, carry):
        over_y(0, 0).wait_send()
        gather_y(0, 0).wait_send()
        return carry

    def left_own(t, carry):
        to_owner(1, 0, 0, 0).wait_send()
        return carry

    def left_lag(t, carry):
        share(1).wait_send()
        return carry

    lax.fori_loop(0, sent, left_block, 0)
    lax.fori_loop(0, 12, left_y, 0)
    lax.fori_loop(0, 63, left_own, 0)
    lax.fori_loop(0, 31, left_lag, 0)


def second(turned, weights, terms, out_hbm, lag_ref, out, sem):
    row = lax.broadcasted_iota(jnp.int32, (ROWS, 256), 0)
    lane = lax.broadcasted_iota(jnp.int32, (ROWS, 256), 1)
    keep = (lane % ROWS) == row
    copies = []
    for start in range(0, 375, 64):
        n = min(64, 375 - start)
        spread = jnp.where(keep[None], turned[start : start + n].astype(F32)[:, None, :], 0.0).astype(BF16)
        value = jnp.dot(spread.reshape(n * ROWS, 256), weights[...], preferred_element_type=F32)
        out[start : start + n] = value.astype(BF16).reshape(n, ROWS, 128)
        rows = pl.ds(start, n)
        copies.append(pltpu.make_async_copy(out.at[rows], out_hbm.at[rows], sem.at[start // 64]))
        copies[-1].start()
    lag_ref[...] = terms[...]
    for copy in copies:
        copy.wait()


def on_device(density, cholesky, virtual_orbitals, occupied_orbitals):
    hbm = pl.BlockSpec(memory_space=pltpu.HBM)
    vmem = pl.BlockSpec(memory_space=pltpu.VMEM)
    dma = pltpu.SemaphoreType.DMA
    turned, weights, terms = pl.pallas_call(
        kernel,
        name="density",
        out_shape=(
            jax.ShapeDtypeStruct((375, 256), BF16),
            jax.ShapeDtypeStruct((256, 128), BF16),
            jax.ShapeDtypeStruct((2, 16), F32),
        ),
        in_specs=[hbm] * 4,
        out_specs=(vmem, vmem, vmem),
        scratch_shapes=[
            pltpu.VMEM((4, 8, ROWS, 3600), BF16),
            pltpu.VMEM((900, 3600), BF16),
            pltpu.VMEM((1800, 375), BF16),
            pltpu.VMEM((16, 128), BF16),
            pltpu.VMEM((16, 128), F32),
            pltpu.VMEM((8, WIDE, 375), BF16),
            pltpu.VMEM((2, 8, ROWS, WIDE), F32),
            pltpu.VMEM((4, NY - 1, 128, WIDE), BF16),
            pltpu.VMEM((4, 128, WIDE), F32),
            pltpu.VMEM((4, NY - 1, 128, WIDE), BF16),
            pltpu.VMEM((4, 8, ROWS, WIDE), BF16),
            pltpu.VMEM((4, 2, 8, ROWS, WIDE), BF16),
            pltpu.VMEM((4, NY, 8, ROWS, WIDE), BF16),
            pltpu.VMEM((2, 16, 128), F32),
            pltpu.VMEM((2, 128), F32),
            pltpu.VMEM((32, 2, 128), F32),
            dma((3,)),
            dma,
            dma((2, 4, 8)),
            dma((4, NY - 1)),
            dma((4,)),
            dma((4, NY - 1)),
            dma,
            pltpu.SemaphoreType.REGULAR((4,)),
            dma,
            dma,
            dma,
            dma,
            dma,
            dma,
        ],
        compiler_params=pltpu.CompilerParams(collective_id=0, has_side_effects=True, vmem_limit_bytes=58 * 2**20),
        cost_estimate=pl.CostEstimate(flops=5 * 10**9, bytes_accessed=12 * 2**20, transcendentals=0),
    )(density.T, cholesky, virtual_orbitals.T, occupied_orbitals.T)
    back, lagrangian = pl.pallas_call(
        second,
        name="second",
        out_shape=(jax.ShapeDtypeStruct((375, ROWS, 128), BF16), jax.ShapeDtypeStruct((2, 16), F32)),
        in_specs=[vmem] * 3,
        out_specs=(hbm, vmem),
        scratch_shapes=[pltpu.VMEM((375, ROWS, 128), BF16), dma((6,))],
        compiler_params=pltpu.CompilerParams(vmem_limit_bytes=60 * 2**20),
        cost_estimate=pl.CostEstimate(flops=4 * 10**8, bytes_accessed=2 * 2**20, transcendentals=0),
    )(turned, weights, terms)
    return back.transpose(1, 2, 0), lagrangian.T


def solution(mesh):
    return jax.shard_map(
        on_device,
        mesh=mesh,
        in_specs=(P("aux", "pair"), P("pair", "aux"), P("aux", None), P()),
        out_specs=(P("pair", None, "aux"), P(None, "aux")),
        check_vma=False,
    )
```
